32 devices in a mesh: fsdp: 4 (over y, core), expert: 8 (over z, x).
Axes of the slice: x: 2, y: 2, z: 4, core: 2. Of those that a mesh axis runs over, the one named last changes fastest.
Arguments:
- tokens: bfloat16 [4096, 1024], P(('fsdp', 'expert')), may hold values from -6 to 6
- expert_ids: int32 [4096, 2], P(('fsdp', 'expert')), may hold values from 0 to 7, all different within a row; in each aligned block of 128 rows (0 to 127, 128 to 255, ...) at most 64 rows name the same one
- gate_weights: float32 [4096, 2], P(('fsdp', 'expert')), may hold values from 0.2 to 1
- weight_in: bfloat16 [8, 2048, 1024], P('expert', 'fsdp'), may hold values from -0.1875 to 0.1875
- weight_out: bfloat16 [8, 2048, 1024], P('expert', 'fsdp'), may hold values from -0.125 to 0.125
- cotangent: bfloat16 [4096, 1024], P(('fsdp', 'expert')), may hold values from -3 to 3
Outputs:
- layer_out: bfloat16 [4096, 1024], P(('fsdp', 'expert'))
- token_grad: bfloat16 [4096, 1024], P(('fsdp', 'expert'))
- grad_in: float32 [8, 2048, 1024], P('expert', 'fsdp')
- grad_out: float32 [8, 2048, 1024], P('expert', 'fsdp')
The draws below stay inside these ranges and needn't reach their ends.
Inputs may be any that keep to these rules, and one draw needn't show every extreme that they name: `expert_ids`: the two experts of a token differ. Among the 128 tokens of one device no expert is chosen by more than 64 tokens, and some device has an expert chosen by exactly 64 tokens.
All inputs are finite; a program needn't handle non-finite values.
Results may differ from the reference program's by a relative error of at most 0.014.
Values may be sent and summed in bfloat16 or wider, within the bound.
A program may use at most 128 MiB of HBM per device.

```python
import math
import jax
import jax.numpy as jnp
import numpy as np
from jax import lax

D = 1024
HID = 2048
TOK_DEV = 128
EXPERTS = 8
CAP = 64
TOKENS = 4096
N_FSDP = 4


def level_of(own_key, dims, cuts, smallest, largest):
    factor_of = 1.0
    for dim, parts in cuts:
        steps = jax.random.uniform(jax.random.fold_in(jax.random.fold_in(own_key, 6), dim), (parts,), jnp.float32, smallest / len(cuts), largest / len(cuts))
        factor_of = factor_of * jnp.repeat(jnp.exp(steps), dims[dim] // parts).reshape((-1,) + (1,) * (len(dims) - 1 - dim))
    return factor_of


def deal_out(own_key, own, number, rows, number_of, top, limit, lean):
    order = jax.random.permutation(own_key, number_of)
    packed, ordinary = portions_of(number_of, rows * top, limit, lean, True), portions_of(number_of, rows * top, limit, lean, False)
    places = jnp.arange(number_of)

    def named(lengths, turn):
        used = int((lengths > 0).sum())
        fixed = max(1, used // 4)
        shifted = fixed + (places - fixed + turn * (used - fixed)) % max(1, number_of - fixed)
        return jnp.zeros((number_of,), jnp.int32).at[order[jnp.where(places < fixed, places, shifted)]].set(jnp.asarray(lengths, jnp.int32))

    lengths = jnp.where(number % 4 == 0, named(packed, number // 4), named(ordinary, number - number // 4 - 1))
    mixed = jax.random.permutation(jax.random.fold_in(own, 3), number_of)
    donor, sink = mixed[0:number_of // 2 * 2:2], mixed[1:number_of // 2 * 2:2]
    slack = jnp.minimum(lengths[donor] - 1, limit - lengths[sink]) // 2
    slack = jnp.where((donor == order[0]) | (sink == order[0]) | (lengths[sink] == 0), 0, jnp.maximum(slack, 0))
    shifted = jax.random.randint(jax.random.fold_in(own, 4), (number_of // 2,), 0, 1 << 20) % (slack + 1)
    lengths = lengths.at[donor].add(-shifted).at[sink].add(shifted)
    items = jnp.searchsorted(jnp.cumsum(lengths), jnp.arange(rows * top), side="right").astype(jnp.int32)
    listing = items.reshape(top, rows).T
    listing = listing[jax.random.permutation(jax.random.fold_in(own, 1), rows)]
    turn = jax.random.randint(jax.random.fold_in(own, 2), (rows, 1), 0, top)
    return jnp.take_along_axis(listing, (jnp.arange(top)[None, :] + turn) % top, axis=1)


def portions_of(amount, total, bound, lean, full):
    portions = [(1 << 20) // math.isqrt(rank ** lean) + 1 for rank in range(1, amount + 1)]
    largest = bound if full else min(bound, max(-(-total // amount), total * portions[0] // sum(portions)))
    least = 1 if total - largest >= amount - 1 else 0
    given, surplus = [largest] + [least] * (amount - 1), total - largest - least * (amount - 1)
    while surplus > 0:
        candidates = [i for i in range(1, amount) if given[i] < largest] or [i for i in range(1, amount) if given[i] < bound]
        mass, remaining = sum([portions[i] for i in candidates]), surplus
        for i in candidates:
            extra = min(bound - given[i], max(1, remaining * portions[i] // mass), surplus)
            given[i] = given[i] + extra
            surplus = surplus - extra
    return np.array(given)


def centred(stream_key, shape, scale, most, shards=(), kind=jnp.bfloat16):
    entries = scale * jax.random.normal(stream_key, shape, jnp.float32)
    if shards:
        entries = entries * level_of(stream_key, shape, shards, -0.22, 0.18)
    return jnp.clip(entries, -most, most).astype(kind)


def setup_inputs(seed: int = 0) -> dict:
    keys = jax.random.split(jax.random.key(seed), 7)
    tokens = centred(keys[0], (TOKENS, D), 1.0, 6.0, ((0, 32),))
    expert_ids_keys = jax.random.split(jax.random.fold_in(keys[1], 1), TOKENS // TOK_DEV)
    expert_ids_turns = jax.random.permutation(jax.random.fold_in(keys[1], 3), TOKENS // TOK_DEV)
    expert_ids = jax.vmap(lambda own, number: deal_out(jax.random.fold_in(keys[1], 2), own, number, TOK_DEV, EXPERTS, 2, CAP, 1))(expert_ids_keys, expert_ids_turns).reshape((TOKENS, 2))
    gate_weights = jnp.clip(0.2 + 0.8 * jax.random.uniform(keys[2], (TOKENS, 2), jnp.float32) ** level_of(keys[2], (TOKENS, 2), ((0, 32),), -0.2, 0.2), 0.2, 1.0)
    weight_in = centred(keys[3], (EXPERTS, HID, D), D ** -0.5, 0.1875, ((0, 8), (1, 4)))
    weight_out = centred(keys[4], (EXPERTS, HID, D), HID ** -0.5, 0.125, ((0, 8), (1, 4)))
    cotangent = centred(keys[5], (TOKENS, D), 0.5, 3.0, ((0, 32),))
    return dict(tokens=tokens, expert_ids=expert_ids, gate_weights=gate_weights, weight_in=weight_in, weight_out=weight_out, cotangent=cotangent)


def gelu_back(pre_act, upstream):
    _, pullback = jax.vjp(jax.nn.gelu, pre_act)
    return pullback(upstream)[0]

def reference(tokens, expert_ids, gate_weights, weight_in, weight_out, cotangent):
    groups = TOKENS // TOK_DEV
    per_group = expert_ids.reshape(groups, TOK_DEV, 2)
    labels = jnp.arange(EXPERTS, dtype=jnp.int32)
    hit_count = lax.optimization_barrier(jnp.sum((per_group[:, :, :, None] == labels).astype(jnp.int32), axis=2, dtype=jnp.int32))
    earlier = jnp.cumsum(hit_count, axis=1, dtype=jnp.int32) - hit_count
    slot_ids = jnp.take_along_axis(earlier, per_group, axis=2).astype(jnp.int32)
    group_ids = jnp.broadcast_to(jnp.arange(groups, dtype=jnp.int32)[:, None, None], per_group.shape)
    token_ids = jnp.broadcast_to(jnp.arange(TOKENS, dtype=jnp.int32).reshape(groups, TOK_DEV, 1), per_group.shape)
    table = jnp.zeros((EXPERTS, groups, CAP), jnp.int32).at[per_group, group_ids, slot_ids].set(token_ids)
    filled = jnp.zeros((EXPERTS, groups, CAP), jnp.float32).at[per_group, group_ids, slot_ids].set(1.0)
    gate_table = jnp.zeros((EXPERTS, groups, CAP), jnp.float32).at[per_group, group_ids, slot_ids].set(gate_weights.reshape(groups, TOK_DEV, 2))

    def one_expert(index):
        where_rows = table[index].reshape(-1)
        live = filled[index].reshape(-1, 1)
        expert_rows = jnp.where(live > 0, tokens[where_rows], jnp.zeros((), jnp.bfloat16))
        activation = jnp.dot(expert_rows, weight_in[index].T, preferred_element_type=jnp.float32)
        hidden = jax.nn.gelu(activation).astype(jnp.bfloat16)
        stored = activation.astype(jnp.bfloat16)
        expert_out = jnp.dot(hidden, weight_out[index], preferred_element_type=jnp.float32).astype(jnp.bfloat16)
        grad_rows = (cotangent[where_rows].astype(jnp.float32) * gate_table[index].reshape(-1, 1)).astype(jnp.bfloat16)
        grad_hidden = jnp.dot(grad_rows, weight_out[index].T, preferred_element_type=jnp.float32)
        grad_act = gelu_back(stored.astype(jnp.float32), grad_hidden).astype(jnp.bfloat16)
        grad_rows_in = jnp.dot(grad_act, weight_in[index], preferred_element_type=jnp.float32).astype(jnp.bfloat16)
        rows_split = expert_rows.reshape(N_FSDP, -1, D).astype(jnp.float32)
        act_split = grad_act.reshape(N_FSDP, -1, HID).astype(jnp.float32)
        hid_split = hidden.reshape(N_FSDP, -1, HID).astype(jnp.float32)
        grad_split = grad_rows.reshape(N_FSDP, -1, D).astype(jnp.float32)
        part_in = jnp.einsum('frh,frd->fhd', act_split, rows_split, precision=lax.Precision.HIGHEST)
        part_out = jnp.einsum('frh,frd->fhd', hid_split, grad_split, precision=lax.Precision.HIGHEST)
        part_in = lax.optimization_barrier(part_in.astype(jnp.bfloat16)).astype(jnp.float32).sum(0)
        part_out = lax.optimization_barrier(part_out.astype(jnp.bfloat16)).astype(jnp.float32).sum(0)
        return (expert_out, grad_rows_in, part_in, part_out)
    expert_out, grad_rows_in, grad_in, grad_out = lax.map(one_expert, jnp.arange(EXPERTS, dtype=jnp.int32))
    flat_index = (per_group * (groups * CAP) + group_ids * CAP + slot_ids).reshape(TOKENS, 2)
    picked = expert_out.reshape(-1, D)[flat_index].astype(jnp.float32)
    layer_out = lax.optimization_barrier(jnp.sum(picked * gate_weights[:, :, None], axis=1)).astype(jnp.bfloat16)
    picked_grad = grad_rows_in.reshape(-1, D)[flat_index].astype(jnp.float32)
    token_grad = lax.optimization_barrier(jnp.sum(picked_grad, axis=1)).astype(jnp.bfloat16)
    return (layer_out, token_grad, grad_in, grad_out)
```

```python
import jax
import jax.numpy as jnp
from jax import lax
from jax.sharding import PartitionSpec as P


def gelu_back(pre_act, upstream):
    _, pullback = jax.vjp(jax.nn.gelu, pre_act)
    return pullback(upstream)[0]


def per_device(tokens, expert_ids, gate_weights, weight_in, weight_out, cotangent):
    tok_count, width = tokens.shape
    expert_count = lax.axis_size("expert")
    capacity = 4 * tok_count // expert_count
    labels = jnp.arange(expert_count, dtype=jnp.int32)
    hit_count = jnp.sum(
        (expert_ids[:, :, None] == labels).astype(jnp.int32), axis=1, dtype=jnp.int32
    )
    order = jnp.arange(tok_count, dtype=jnp.int32)
    before = (order[:, None] > order[None, :]).astype(jnp.bfloat16)
    earlier = jnp.dot(before, hit_count.astype(jnp.bfloat16), preferred_element_type=jnp.float32)
    slot_ids = jnp.sum(
        jnp.where(expert_ids[:, :, None] == labels, earlier[:, None, :], 0.0), axis=2
    ).astype(jnp.int32)
    target = expert_ids * capacity + slot_ids
    cell_ids = jnp.arange(expert_count * capacity, dtype=jnp.int32)[:, None]
    first_hit = cell_ids == target[:, 0][None, :]
    second_hit = cell_ids == target[:, 1][None, :]
    placing = (first_hit | second_hit).astype(jnp.bfloat16)
    gate_cells = jnp.sum(
        jnp.where(first_hit, gate_weights[:, 0][None, :], 0.0)
        + jnp.where(second_hit, gate_weights[:, 1][None, :], 0.0),
        axis=1,
    )
    outgoing = jnp.dot(placing, tokens, preferred_element_type=jnp.float32).astype(jnp.bfloat16)
    arrived = lax.all_to_all(
        outgoing.reshape(expert_count, capacity, width),
        "expert",
        split_axis=0,
        concat_axis=0,
        tiled=True,
    )
    expert_rows = arrived.reshape(-1, width)
    pieces = (
        lax.all_gather(weight_in, "fsdp", axis=1, tiled=True),
        lax.all_gather(weight_out, "fsdp", axis=1, tiled=True),
    )
    full_in = None
    full_out = None
    part_in = pieces[0][0]
    part_out = pieces[1][0]
    activation = lax.dot_general(
        expert_rows, part_in, (((1,), (1,)), ((), ())), preferred_element_type=jnp.float32
    )
    hidden = jax.nn.gelu(activation).astype(jnp.bfloat16)
    summed = jnp.dot(hidden, part_out, preferred_element_type=jnp.float32)
    forward_stored = activation.astype(jnp.bfloat16)
    summed, stored, hidden_buf, full_in, full_out = (
        summed,
        forward_stored,
        hidden,
        full_in,
        full_out,
    )
    expert_out = summed.astype(jnp.bfloat16).reshape(expert_count, capacity, width)
    returned = lax.all_to_all(
        expert_out, "expert", split_axis=0, concat_axis=0, tiled=True
    ).reshape(-1, width)
    picked = returned[target].astype(jnp.float32)
    layer_out = jnp.sum(picked * gate_weights[:, :, None], axis=1).astype(jnp.bfloat16)
    grad_cells = (
        jnp.dot(placing, cotangent, preferred_element_type=jnp.float32) * gate_cells[:, None]
    )
    grad_cells = grad_cells.astype(jnp.bfloat16).reshape(expert_count, capacity, width)
    grad_rows = lax.all_to_all(
        grad_cells, "expert", split_axis=0, concat_axis=0, tiled=True
    ).reshape(-1, width)
    pieces = (
        lax.all_gather(weight_in, "fsdp", axis=1, tiled=True),
        lax.all_gather(weight_out, "fsdp", axis=1, tiled=True),
    )
    part_in = pieces[0][0]
    part_out = pieces[1][0]
    grad_hidden = lax.dot_general(
        grad_rows, part_out, (((1,), (1,)), ((), ())), preferred_element_type=jnp.float32
    )
    pre_act = stored.astype(jnp.float32)
    grad_act = gelu_back(pre_act, grad_hidden).astype(jnp.bfloat16)
    summed_grad = jnp.dot(grad_act, part_in, preferred_element_type=jnp.float32)
    summed_grad, grad_act_buf = (summed_grad, grad_act)
    grad_back = summed_grad.astype(jnp.bfloat16).reshape(expert_count, capacity, width)
    grad_returned = lax.all_to_all(
        grad_back, "expert", split_axis=0, concat_axis=0, tiled=True
    ).reshape(-1, width)
    token_grad = jnp.sum(grad_returned[target].astype(jnp.float32), axis=1).astype(jnp.bfloat16)
    both_shards = lax.psum_scatter(
        jnp.concatenate(
            [
                lax.dot_general(
                    grad_act_buf,
                    expert_rows,
                    (((0,), (0,)), ((), ())),
                    preferred_element_type=jnp.float32,
                ),
                lax.dot_general(
                    hidden_buf,
                    grad_rows,
                    (((0,), (0,)), ((), ())),
                    preferred_element_type=jnp.float32,
                ),
            ],
            axis=1,
        ).astype(jnp.bfloat16),
        "fsdp",
        scatter_dimension=0,
        tiled=True,
    ).astype(jnp.float32)
    grad_in_shard = both_shards[:, :width]
    grad_out_shard = both_shards[:, width:]
    return (layer_out, token_grad, grad_in_shard[None], grad_out_shard[None])


def solution(mesh):
    return jax.shard_map(
        per_device,
        mesh=mesh,
        in_specs=(
            P(("fsdp", "expert"), None),
            P(("fsdp", "expert"), None),
            P(("fsdp", "expert"), None),
            P("expert", "fsdp", None),
            P("expert", "fsdp", None),
            P(("fsdp", "expert"), None),
        ),
        out_specs=(
            P(("fsdp", "expert"), None),
            P(("fsdp", "expert"), None),
            P("expert", "fsdp", None),
            P("expert", "fsdp", None),
        ),
        check_vma=False,
    )
```

```python
import functools
import math

import jax
import jax.numpy as jnp
from jax import lax
from jax.experimental import pallas as pl
from jax.experimental.pallas import tpu as pltpu
from jax.sharding import PartitionSpec as P

F32, BF16 = jnp.float32, jnp.bfloat16
NN = (((1,), (0,)), ((), ()))
NT = (((1,), (1,)), ((), ()))
TN = (((0,), (0,)), ((), ()))


def mul(a, b, dims):
    return lax.dot_general(a, b, dims, preferred_element_type=F32)


def kernel(
    n_f, n_e, cap, steps, depth,
    win, wout, tok, cot, ids, gates,
    layer_out, token_grad, grad_in, grad_out,
    wall, x_send, g_send, x_rows, g_rows, hid, slope, out_acc, dx_acc,
    out_send, dx_send, out_back, dx_back, to_sib, from_sib, to_chip, from_chip, marks,
    load_sem, w_send, w_recv, relay_send, a_send, a_recv, s_send, s_recv, c_send, c_recv,
):
    f, e = lax.axis_index("fsdp"), lax.axis_index("expert")
    chip, core = f // 2, lax.rem(f, 2)
    chips = n_f // 2
    sib = chip * 2 + 1 - core
    count = tok.shape[0]
    cells = n_e * cap

    def over_there(j):
        return lax.rem(chip + j, chips)

    def before(j):
        return lax.rem(chip - j + chips, chips)

    def load(t, a):
        src = win if a == 0 else wout
        return pltpu.make_async_copy(
            src.at[pl.ds(t * depth, depth)], wall.at[f, t, a], load_sem.at[t, a]
        )

    for t in range(steps):
        for a in range(2):
            load(t, a).start()

    barrier = pltpu.get_barrier_semaphore()

    def signal(fi, ei):
        pl.semaphore_signal(
            barrier, inc=1, device_id=(fi, ei), device_id_type=pl.DeviceIdType.MESH
        )

    signal(sib, e)
    for j in range(1, chips):
        signal(over_there(j) * 2 + core, e)

    @pl.loop(1, n_e)
    def _(k):
        signal(f, lax.rem(e + k, n_e))

    def remote(src, dst, send, recv, fi, ei):
        return pltpu.make_async_remote_copy(
            src_ref=src, dst_ref=dst, send_sem=send, recv_sem=recv,
            device_id=(fi, ei), device_id_type=pl.DeviceIdType.MESH,
        )

    def share(t, j):
        to = sib if j == 0 else over_there(j) * 2 + core
        return remote(wall.at[f, t], wall.at[f, t], w_send.at[j, t], w_recv.at[f, t], to, e)

    def arrival(s, t):
        return remote(wall.at[s, t], wall.at[s, t], w_send.at[0, t], w_recv.at[s, t], sib, e)

    def relay(s, t, j):
        return remote(wall.at[s, t], wall.at[s, t], relay_send.at[j, t], w_recv.at[s, t], sib, e)

    pl.semaphore_wait(barrier, 1 + (chips - 1) + (n_e - 1))
    for t in range(steps):
        for a in range(2):
            load(t, a).wait()
        for j in range(1, chips):
            share(t, j).start()
        share(t, 0).start()

    lanes = lax.broadcasted_iota(jnp.int32, (count, 128), 1)
    first, second = ids[:, 0:1], ids[:, 1:2]
    hit = (lanes == first).astype(F32) + (lanes == second).astype(F32)
    earlier_than = (
        lax.broadcasted_iota(jnp.int32, (count, count), 0)
        > lax.broadcasted_iota(jnp.int32, (count, count), 1)
    ).astype(F32)
    earlier = mul(earlier_than.astype(BF16), hit.astype(BF16), NN)
    spots = lax.broadcasted_iota(jnp.int32, (count, cells), 1)
    gate_at = jnp.zeros((count, cells), F32)
    placed = jnp.zeros((count, cells), F32)
    for k, chosen in enumerate((first, second)):
        slot = jnp.sum(jnp.where(lanes == chosen, earlier, 0.0), axis=1, keepdims=True)
        here = spots == chosen * cap + slot.astype(jnp.int32)
        marks[k] = here.astype(F32).astype(BF16)
        placed += here.astype(F32)
        gate_at += jnp.where(here, gates[:, k : k + 1], 0.0)
    placing = placed.T.astype(BF16)
    gate_cells = jnp.sum(gate_at.T, axis=1, keepdims=True)

    def part(buf, i):
        return buf.at[pl.ds(pl.multiple_of(i * cap, cap), cap)]

    def exchange(a, src, dst, k):
        to = lax.rem(e + k, n_e)
        return remote(part(src, to), part(dst, e), a_send.at[a, k], a_recv.at[a, k], f, to)

    def arriving(a, src, dst, k):
        frm = lax.rem(e - k + n_e, n_e)
        return remote(part(src, frm), part(dst, frm), a_send.at[a, k], a_recv.at[a, k], f, frm)

    def send_all(a, src, dst):
        @pl.loop(1, n_e)
        def _(k):
            exchange(a, src, dst, k).start()

        own = pl.ds(pl.multiple_of(e * cap, cap), cap)
        dst[own, :] = src[own, :]

    def receive_all(a, src, dst):
        @pl.loop(1, n_e)
        def _(k):
            arriving(a, src, dst, k).wait_recv()

    def sent_all(a, src, dst):
        @pl.loop(1, n_e)
        def _(k):
            exchange(a, src, dst, k).wait_send()

    x_send[...] = mul(placing, tok[...], NN).astype(BF16)
    send_all(0, x_send, x_rows)
    g_send[...] = (mul(placing, cot[...], NN) * gate_cells).astype(BF16)
    send_all(1, g_send, g_rows)
    out_acc[...] = jnp.zeros_like(out_acc)
    dx_acc[...] = jnp.zeros_like(dx_acc)

    scale = math.sqrt(2.0 / math.pi)

    def forward(s, t):
        pre = mul(x_rows[...], wall[s, t, 0], NT)
        square = pre * pre
        th = jnp.tanh(scale * pre * (1.0 + 0.044715 * square))
        half = 0.5 * (1.0 + th)
        hidden = (pre * half).astype(BF16)
        hid[s, t] = hidden
        slope[s, t] = half + 0.5 * pre * (1.0 - th * th) * (
            scale * (1.0 + 3.0 * 0.044715 * square)
        )
        out_acc[...] += mul(hidden, wall[s, t, 1], NN)

    receive_all(0, x_send, x_rows)

    @pl.loop(0, steps)
    def _(t):
        forward(f, t)

    @pl.loop(0, steps)
    def _(t):
        arrival(sib, t).wait_recv()
        forward(sib, t)

    @pl.loop(1, chips)
    def _(j):
        s = over_there(j) * 2 + core

        @pl.loop(0, steps)
        def _(t):
            arrival(s, t).wait_recv()
            relay(s, t, j).start()
            forward(s, t)

    @pl.loop(1, chips)
    def _(j):
        s = over_there(j) * 2 + 1 - core

        @pl.loop(0, steps)
        def _(t):
            arrival(s, t).wait_recv()
            forward(s, t)

    out_send[...] = out_acc[...].astype(BF16)
    send_all(2, out_send, out_back)

    def backward(s, t):
        d_hidden = mul(g_rows[...], wall[s, t, 1], NT)
        d_pre = (d_hidden * slope[s, t]).astype(BF16)
        dx_acc[...] += mul(d_pre, wall[s, t, 0], NN)
        return mul(d_pre, x_rows[...], TN), mul(hid[s, t], g_rows[...], TN)

    def to_sibling(j, t):
        return remote(to_sib.at[j, t], from_sib.at[j, t], s_send.at[j, t], s_recv.at[j, t], sib, e)

    def across(j, t):
        to = over_there(j) * 2 + core
        return remote(to_chip.at[j, t], from_chip.at[j, t], c_send.at[j, t], c_recv.at[j, t], to, e)

    def across_in(j, t):
        frm = before(j) * 2 + core
        return remote(to_chip.at[j, t], from_chip.at[j, t], c_send.at[j, t], c_recv.at[j, t], frm, e)

    receive_all(1, g_send, g_rows)

    def siblings(j):
        s = over_there(j) * 2 + 1 - core

        @pl.loop(0, steps)
        def _(t):
            g_in, g_out = backward(s, t)
            to_sib[j, t, 0] = g_in.astype(BF16)
            to_sib[j, t, 1] = g_out.astype(BF16)
            to_sibling(j, t).start()

    @pl.loop(1, chips)
    def _(j):
        siblings(j)

    @pl.loop(1, chips)
    def _(j):
        s = over_there(j) * 2 + core

        @pl.loop(0, steps)
        def _(t):
            g_in, g_out = backward(s, t)
            to_sibling(j, t).wait_recv()
            to_chip[j, t, 0] = (g_in + from_sib[j, t, 0].astype(F32)).astype(BF16)
            to_chip[j, t, 1] = (g_out + from_sib[j, t, 1].astype(F32)).astype(BF16)
            across(j, t).start()

    siblings(0)

    @pl.loop(0, steps)
    def _(t):
        g_in, g_out = backward(f, t)
        rows = pl.ds(pl.multiple_of(t * depth, depth), depth)
        grad_in[rows, :] = g_in
        grad_out[rows, :] = g_out

    dx_send[...] = dx_acc[...].astype(BF16)
    send_all(3, dx_send, dx_back)

    @pl.loop(0, steps)
    def _(t):
        to_sibling(0, t).wait_recv()
        rows = pl.ds(pl.multiple_of(t * depth, depth), depth)
        grad_in[rows, :] += from_sib[0, t, 0].astype(F32)
        grad_out[rows, :] += from_sib[0, t, 1].astype(F32)

    receive_all(2, out_send, out_back)
    layer_out[...] = (
        mul(marks[0], out_back[...], NN) * gates[:, 0:1]
        + mul(marks[1], out_back[...], NN) * gates[:, 1:2]
    ).astype(BF16)

    @pl.loop(1, chips)
    def _(j):
        @pl.loop(0, steps)
        def _(t):
            across_in(j, t).wait_recv()
            rows = pl.ds(pl.multiple_of(t * depth, depth), depth)
            grad_in[rows, :] += from_chip[j, t, 0].astype(F32)
            grad_out[rows, :] += from_chip[j, t, 1].astype(F32)

    receive_all(3, dx_send, dx_back)
    token_grad[...] = (
        mul(marks[0], dx_back[...], NN) + mul(marks[1], dx_back[...], NN)
    ).astype(BF16)

    for a, (src, dst) in enumerate(
        ((x_send, x_rows), (g_send, g_rows), (out_send, out_back), (dx_send, dx_back))
    ):
        sent_all(a, src, dst)
    for t in range(steps):
        for j in range(chips):
            share(t, j).wait_send()
            to_sibling(j, t).wait_send()
        for j in range(1, chips):
            relay(over_there(j) * 2 + core, t, j).wait_send()
            across(j, t).wait_send()


def per_device(tokens, expert_ids, gate_weights, weight_in, weight_out, cotangent):
    count, width = tokens.shape
    n_f, n_e = lax.axis_size("fsdp"), lax.axis_size("expert")
    cap = 4 * count // n_e
    owned = weight_in.shape[1]
    depth = min(256, owned)
    steps = owned // depth
    rows, chips = n_e * cap, n_f // 2
    vmem = pl.BlockSpec(memory_space=pltpu.VMEM)
    anywhere = pl.BlockSpec(memory_space=pl.ANY)
    dma = pltpu.SemaphoreType.DMA
    wide = pltpu.VMEM((rows, width), BF16)
    total = pltpu.VMEM((rows, width), F32)
    pieces = pltpu.VMEM((chips, steps, 2, depth, width), BF16)
    flops = 12 * rows * width * owned * n_f
    layer_out, token_grad, grad_in, grad_out = pl.pallas_call(
        functools.partial(kernel, n_f, n_e, cap, steps, depth),
        out_shape=(
            jax.ShapeDtypeStruct((count, width), BF16),
            jax.ShapeDtypeStruct((count, width), BF16),
            jax.ShapeDtypeStruct((owned, width), F32),
            jax.ShapeDtypeStruct((owned, width), F32),
        ),
        in_specs=[anywhere, anywhere, vmem, vmem, vmem, vmem],
        out_specs=(vmem, vmem, vmem, vmem),
        scratch_shapes=[
            pltpu.VMEM((n_f, steps, 2, depth, width), BF16),
            wide, wide, wide, wide,
            pltpu.VMEM((n_f, steps, rows, depth), BF16),
            pltpu.VMEM((n_f, steps, rows, depth), F32),
            total, total,
            wide, wide, wide, wide,
            pieces, pieces, pieces, pieces,
            pltpu.VMEM((2, count, rows), BF16),
            dma((steps, 2)),
            dma((chips, steps)),
            dma((n_f, steps)),
            dma((chips, steps)),
            dma((4, n_e)),
            dma((4, n_e)),
            dma((chips, steps)),
            dma((chips, steps)),
            dma((chips, steps)),
            dma((chips, steps)),
        ],
        compiler_params=pltpu.CompilerParams(
            collective_id=0, has_side_effects=True, vmem_limit_bytes=58 * 2**20
        ),
        cost_estimate=pl.CostEstimate(
            flops=flops, bytes_accessed=16 * owned * width, transcendentals=rows * owned * n_f
        ),
    )(weight_in[0], weight_out[0], tokens, cotangent, expert_ids, gate_weights)
    return layer_out, token_grad, grad_in[None], grad_out[None]


def solution(mesh):
    tok, weight = P(("fsdp", "expert"), None), P("expert", "fsdp", None)
    return jax.shard_map(
        per_device,
        mesh=mesh,
        in_specs=(tok, tok, tok, weight, weight, tok),
        out_specs=(tok, tok, weight, weight),
        check_vma=False,
    )
```

```python
import functools
import math

import jax
import jax.numpy as jnp
from jax import lax
from jax.experimental import pallas as pl
from jax.experimental.pallas import tpu as pltpu
from jax.sharding import PartitionSpec as P

F32, BF16 = jnp.float32, jnp.bfloat16
NN = (((1,), (0,)), ((), ()))
NT = (((1,), (1,)), ((), ()))
TN = (((0,), (0,)), ((), ()))


def mul(a, b, dims):
    return lax.dot_general(a, b, dims, preferred_element_type=F32)


def upright(rows):
    return jnp.concatenate([rows, jnp.zeros((6, rows.shape[1]), rows.dtype)], axis=0).T


def kernel(
    n_f, n_e, cap, steps, depth,
    win, wout, tok, cot, ids, gates,
    layer_out, token_grad, grad_in, grad_out,
    wall, x_send, g_send, x_rows, g_rows, hid, slope, out_acc, dx_acc,
    out_send, dx_send, out_back, dx_back, to_sib, from_sib, to_chip, from_chip, marks, gate_at_token, slopes_on,
    load_sem, w_send, w_recv, relay_send, a_send, a_recv, s_send, s_recv, c_send, c_recv,
):
    f, e = lax.axis_index("fsdp"), lax.axis_index("expert")
    chip, core = f // 2, lax.rem(f, 2)
    chips = n_f // 2
    sib = chip * 2 + 1 - core
    count = tok.shape[0]
    cells = n_e * cap

    def over_there(j):
        return lax.rem(chip + j, chips)

    def before(j):
        return lax.rem(chip - j + chips, chips)

    def load(t, a):
        src = win if a == 0 else wout
        return pltpu.make_async_copy(
            src.at[pl.ds(t * depth, depth)], wall.at[f, t, a], load_sem.at[t, a]
        )

    for t in range(steps):
        for a in range(2):
            load(t, a).start()

    barrier = pltpu.get_barrier_semaphore()

    def signal(fi, ei):
        pl.semaphore_signal(
            barrier, inc=1, device_id=(fi, ei), device_id_type=pl.DeviceIdType.MESH
        )

    signal(sib, e)
    for j in range(1, chips):
        signal(over_there(j) * 2 + core, e)

    @pl.loop(1, n_e)
    def _(k):
        signal(f, lax.rem(e + k, n_e))

    def remote(src, dst, send, recv, fi, ei):
        return pltpu.make_async_remote_copy(
            src_ref=src, dst_ref=dst, send_sem=send, recv_sem=recv,
            device_id=(fi, ei), device_id_type=pl.DeviceIdType.MESH,
        )

    def share(t, j):
        to = sib if j == 0 else over_there(j) * 2 + core
        return remote(wall.at[f, t], wall.at[f, t], w_send.at[j, t], w_recv.at[f, t], to, e)

    def arrival(s, t):
        return remote(wall.at[s, t], wall.at[s, t], w_send.at[0, t], w_recv.at[s, t], sib, e)

    def relay(s, t, j):
        return remote(wall.at[s, t], wall.at[s, t], relay_send.at[j, t], w_recv.at[s, t], sib, e)

    ids_at, gate_at_token[...] = upright(ids[...].astype(F32)), upright(gates[...])
    lanes = lax.broadcasted_iota(jnp.int32, (count, 128), 1)
    first, second = ids_at[:, 0:1].astype(jnp.int32), ids_at[:, 1:2].astype(jnp.int32)
    hit = (lanes == first).astype(F32) + (lanes == second).astype(F32)
    earlier_than = (
        lax.broadcasted_iota(jnp.int32, (count, count), 0)
        > lax.broadcasted_iota(jnp.int32, (count, count), 1)
    ).astype(F32)
    earlier = mul(earlier_than.astype(BF16), hit.astype(BF16), NN)
    spots = lax.broadcasted_iota(jnp.int32, (count, cells), 1)
    gate_at = jnp.zeros((count, cells), F32)
    placed = jnp.zeros((count, cells), F32)
    for k, chosen in enumerate((first, second)):
        slot = jnp.sum(jnp.where(lanes == chosen, earlier, 0.0), axis=1, keepdims=True)
        here = spots == chosen * cap + slot.astype(jnp.int32)
        marks[k] = here.astype(F32).astype(BF16)
        placed += here.astype(F32)
        gate_at += jnp.where(here, gate_at_token[:, k : k + 1], 0.0)
    placing = placed.T.astype(BF16)
    gate_cells = jnp.sum(gate_at.T, axis=1, keepdims=True)

    def part(buf, i):
        return buf.at[pl.ds(pl.multiple_of(i * cap, cap), cap)]

    def exchange(a, src, dst, k):
        to = lax.rem(e + k, n_e)
        return remote(part(src, to), part(dst, e), a_send.at[a, k], a_recv.at[a, k], f, to)

    def arriving(a, src, dst, k):
        frm = lax.rem(e - k + n_e, n_e)
        return remote(part(src, frm), part(dst, frm), a_send.at[a, k], a_recv.at[a, k], f, frm)

    def send_all(a, src, dst):
        @pl.loop(1, n_e)
        def _(k):
            exchange(a, src, dst, k).start()

        own = pl.ds(pl.multiple_of(e * cap, cap), cap)
        dst[own, :] = src[own, :]

    def receive_all(a, src, dst):
        @pl.loop(1, n_e)
        def _(k):
            arriving(a, src, dst, k).wait_recv()

    def sent_all(a, src, dst):
        @pl.loop(1, n_e)
        def _(k):
            exchange(a, src, dst, k).wait_send()

    x_send[...] = mul(placing, tok[...], NN).astype(BF16)
    pl.semaphore_wait(barrier, 1 + (chips - 1) + (n_e - 1))
    for t in range(steps):
        for a in range(2):
            load(t, a).wait()
        for j in range(1, chips):
            share(t, j).start()
        share(t, 0).start()
    send_all(0, x_send, x_rows)
    g_send[...] = (mul(placing, cot[...], NN) * gate_cells).astype(BF16)

    @pl.loop(1, n_e)
    def _(k):
        exchange(0, x_send, x_rows, k).wait_send()
        exchange(1, g_send, g_rows, k).start()

    own_cells = pl.ds(pl.multiple_of(e * cap, cap), cap)
    g_rows[own_cells, :] = g_send[own_cells, :]
    out_acc[...] = jnp.zeros_like(out_acc)
    dx_acc[...] = jnp.zeros_like(dx_acc)

    scale = math.sqrt(2.0 / math.pi)

    def forward(s, t):
        pre = mul(x_rows[...], wall[s, t, 0], NT)
        square = pre * pre
        th = jnp.tanh(scale * pre * (1.0 + 0.044715 * square))
        half = 0.5 * (1.0 + th)
        hidden = (pre * half).astype(BF16)
        hid[s, t] = hidden
        slope[s, t] = half + 0.5 * pre * (1.0 - th * th) * (
            scale * (1.0 + 3.0 * 0.044715 * square)
        )
        out_acc[...] += mul(hidden, wall[s, t, 1], NN)

    receive_all(0, x_send, x_rows)

    @pl.loop(0, steps)
    def _(t):
        forward(f, t)

    @pl.loop(0, steps)
    def _(t):
        arrival(sib, t).wait_recv()
        forward(sib, t)

    def take(j, t):
        s = over_there(j) * 2 + core
        arrival(s, t).wait_recv()
        relay(s, t, j).start()

    def forward_there(j, t):
        forward(over_there(j) * 2 + core, t)
        s = over_there(j) * 2 + 1 - core
        arrival(s, t).wait_recv()
        forward(s, t)

    @pl.loop(1, chips)
    def _(j):
        take(j, 0)
        forward_there(j, 0)

    def back(s, t):
        d_hidden = mul(g_rows[...], wall[s, t, 1], NT)
        d_pre = (d_hidden * slope[s, t]).astype(BF16)
        dx_acc[...] += mul(d_pre, wall[s, t, 0], NN)
        return d_pre

    def weight_grads(s, t, d_pre):
        return mul(d_pre, x_rows[...], TN), mul(hid[s, t], g_rows[...], TN)

    def backward(s, t):
        return weight_grads(s, t, back(s, t))

    def to_sibling(j, t):
        return remote(to_sib.at[j, t], from_sib.at[j, t], s_send.at[j, t], s_recv.at[j, t], sib, e)

    def across(j, t):
        to = over_there(j) * 2 + core
        return remote(to_chip.at[j, t], from_chip.at[j, t], c_send.at[j, t], c_recv.at[j, t], to, e)

    def across_in(j, t):
        frm = before(j) * 2 + core
        return remote(to_chip.at[j, t], from_chip.at[j, t], c_send.at[j, t], c_recv.at[j, t], frm, e)

    def pass_on(j, t, g_in, g_out):
        to_sib[j, t, 0] = g_in.astype(BF16)
        to_sib[j, t, 1] = g_out.astype(BF16)
        to_sibling(j, t).start()

    def backward_there(j, t):
        g_in, g_out = backward(over_there(j) * 2 + 1 - core, t)
        pass_on(j, t, g_in, g_out)
        g_in, g_out = backward(over_there(j) * 2 + core, t)
        to_sibling(j, t).wait_recv()
        to_chip[j, t, 0] = (g_in + from_sib[j, t, 0].astype(F32)).astype(BF16)
        to_chip[j, t, 1] = (g_out + from_sib[j, t, 1].astype(F32)).astype(BF16)
        across(j, t).start()

    receive_all(1, g_send, g_rows)

    @pl.loop(1, chips)
    def _(j):
        backward_there(j, 0)

    @pl.loop(1, steps)
    def _(t):
        @pl.loop(1, chips)
        def _(j):
            take(j, t)

        @pl.loop(1, chips)
        def _(j):
            forward_there(j, t)

    out_send[...] = out_acc[...].astype(BF16)
    send_all(2, out_send, out_back)

    @pl.loop(1, steps)
    def _(t):
        @pl.loop(1, chips)
        def _(j):
            backward_there(j, t)

    for i, s in enumerate((sib, f)):

        @pl.loop(0, steps)
        def _(t, i=i, s=s):
            slopes_on[i, t] = back(s, t)

    dx_send[...] = dx_acc[...].astype(BF16)
    send_all(3, dx_send, dx_back)

    @pl.loop(0, steps)
    def _(t):
        g_in, g_out = weight_grads(sib, t, slopes_on[0, t])
        pass_on(0, t, g_in, g_out)

    @pl.loop(0, steps)
    def _(t):
        g_in, g_out = weight_grads(f, t, slopes_on[1, t])
        rows = pl.ds(pl.multiple_of(t * depth, depth), depth)
        grad_in[rows, :] = g_in
        grad_out[rows, :] = g_out

    @pl.loop(0, steps)
    def _(t):
        to_sibling(0, t).wait_recv()
        rows = pl.ds(pl.multiple_of(t * depth, depth), depth)
        grad_in[rows, :] += from_sib[0, t, 0].astype(F32)
        grad_out[rows, :] += from_sib[0, t, 1].astype(F32)

    receive_all(2, out_send, out_back)
    layer_out[...] = (
        mul(marks[0], out_back[...], NN) * gate_at_token[:, 0:1]
        + mul(marks[1], out_back[...], NN) * gate_at_token[:, 1:2]
    ).astype(BF16)

    @pl.loop(1, chips)
    def _(j):
        @pl.loop(0, steps)
        def _(t):
            across_in(j, t).wait_recv()
            rows = pl.ds(pl.multiple_of(t * depth, depth), depth)
            grad_in[rows, :] += from_chip[j, t, 0].astype(F32)
            grad_out[rows, :] += from_chip[j, t, 1].astype(F32)

    receive_all(3, dx_send, dx_back)
    token_grad[...] = (
        mul(marks[0], dx_back[...], NN) + mul(marks[1], dx_back[...], NN)
    ).astype(BF16)

    sent_all(1, g_send, g_rows)
    sent_all(2, out_send, out_back)
    sent_all(3, dx_send, dx_back)
    for t in range(steps):
        for j in range(chips):
            share(t, j).wait_send()
            to_sibling(j, t).wait_send()
        for j in range(1, chips):
            relay(over_there(j) * 2 + core, t, j).wait_send()
            across(j, t).wait_send()


def settle(cuts, sources, targets, sems):
    copies = []
    for i, (src, dst) in enumerate(zip(sources, targets)):
        rows = src.shape[0] // cuts[i]
        for c in range(cuts[i]):
            part = pl.ds(c * rows, rows)
            copies.append(
                pltpu.make_async_copy(src.at[part], dst.at[part], sems.at[len(copies)])
            )
    for copy in copies:
        copy.start()
    for copy in copies:
        copy.wait()


def per_device(tokens, expert_ids, gate_weights, weight_in, weight_out, cotangent):
    count, width = tokens.shape
    n_f, n_e = lax.axis_size("fsdp"), lax.axis_size("expert")
    cap = 4 * count // n_e
    owned = weight_in.shape[1]
    depth = min(256, owned)
    steps = owned // depth
    rows, chips = n_e * cap, n_f // 2
    vmem = pl.BlockSpec(memory_space=pltpu.VMEM)
    anywhere = pl.BlockSpec(memory_space=pl.ANY)
    dma = pltpu.SemaphoreType.DMA
    wide = pltpu.VMEM((rows, width), BF16)
    total = pltpu.VMEM((rows, width), F32)
    pieces = pltpu.VMEM((chips, steps, 2, depth, width), BF16)
    flops = 12 * rows * width * owned * n_f
    layer_out, token_grad, grad_in, grad_out = pl.pallas_call(
        functools.partial(kernel, n_f, n_e, cap, steps, depth),
        out_shape=(
            jax.ShapeDtypeStruct((count, width), BF16),
            jax.ShapeDtypeStruct((count, width), BF16),
            jax.ShapeDtypeStruct((owned, width), F32),
            jax.ShapeDtypeStruct((owned, width), F32),
        ),
        in_specs=[anywhere, anywhere, vmem, vmem, vmem, vmem],
        out_specs=(vmem, vmem, vmem, vmem),
        scratch_shapes=[
            pltpu.VMEM((n_f, steps, 2, depth, width), BF16),
            wide, wide, wide, wide,
            pltpu.VMEM((n_f, steps, rows, depth), BF16),
            pltpu.VMEM((n_f, steps, rows, depth), F32),
            total, total,
            wide, wide, wide, wide,
            pieces, pieces, pieces, pieces,
            pltpu.VMEM((2, count, rows), BF16),
            pltpu.VMEM((count, 8), F32),
            pltpu.VMEM((2, steps, rows, depth), BF16),
            dma((steps, 2)),
            dma((chips, steps)),
            dma((n_f, steps)),
            dma((chips, steps)),
            dma((4, n_e)),
            dma((4, n_e)),
            dma((chips, steps)),
            dma((chips, steps)),
            dma((chips, steps)),
            dma((chips, steps)),
        ],
        compiler_params=pltpu.CompilerParams(
            collective_id=0, has_side_effects=True, vmem_limit_bytes=58 * 2**20
        ),
        cost_estimate=pl.CostEstimate(
            flops=flops, bytes_accessed=16 * owned * width, transcendentals=rows * owned * n_f
        ),
    )(weight_in[0], weight_out[0], tokens, cotangent, expert_ids.T, gate_weights.T)
    results = (layer_out, token_grad, grad_in, grad_out)
    cuts = (1, 1, 4, 4)
    layer_out, token_grad, grad_in, grad_out = pl.pallas_call(
        lambda *refs: settle(cuts, refs[:4], refs[4:8], refs[8]),
        out_shape=tuple(jax.ShapeDtypeStruct(r.shape, r.dtype) for r in results),
        in_specs=[anywhere] * 4,
        out_specs=(anywhere,) * 4,
        scratch_shapes=[dma((sum(cuts),))],
    )(*results)
    return layer_out, token_grad, grad_in[None], grad_out[None]


def solution(mesh):
    tok, weight = P(("fsdp", "expert"), None), P("expert", "fsdp", None)
    return jax.shard_map(
        per_device,
        mesh=mesh,
        in_specs=(tok, tok, tok, weight, weight, tok),
        out_specs=(tok, tok, weight, weight),
        check_vma=False,
    )
```

```python
import functools
import math

import jax
import jax.numpy as jnp
from jax import lax
from jax.experimental import pallas as pl
from jax.experimental.pallas import tpu as pltpu
from jax.sharding import PartitionSpec as P

F32, BF16 = jnp.float32, jnp.bfloat16
NN = (((1,), (0,)), ((), ()))
NT = (((1,), (1,)), ((), ()))
TN = (((0,), (0,)), ((), ()))


def mul(a, b, dims):
    return lax.dot_general(a, b, dims, preferred_element_type=F32)


def upright(rows):
    return jnp.concatenate([rows, jnp.zeros((6, rows.shape[1]), rows.dtype)], axis=0).T


def kernel(
    n_f, n_e, cap, steps, depth,
    win, wout, tok, cot, ids, gates,
    layer_out, token_grad, grad_in, grad_out,
    wall, x_send, g_send, x_rows, g_rows, hid, slope, out_acc, dx_acc,
    out_send, dx_send, out_back, dx_back, to_sib, from_sib, to_chip, from_chip, marks, gate_at_token, slopes_on,
    load_sem, w_send, w_recv, relay_send, a_send, a_recv, s_send, s_recv, c_send, c_recv,
):
    f, e = lax.axis_index("fsdp"), lax.axis_index("expert")
    chip, core = f // 2, lax.rem(f, 2)
    chips = n_f // 2
    sib = chip * 2 + 1 - core
    count = tok.shape[0]
    cells = n_e * cap

    def over_there(j):
        return lax.rem(chip + j, chips)

    def before(j):
        return lax.rem(chip - j + chips, chips)

    def load(t, a):
        src = win if a == 0 else wout
        return pltpu.make_async_copy(
            src.at[pl.ds(t * depth, depth)], wall.at[f, t, a], load_sem.at[t, a]
        )

    for t in range(steps):
        for a in range(2):
            load(t, a).start()

    barrier = pltpu.get_barrier_semaphore()

    def signal(fi, ei):
        pl.semaphore_signal(
            barrier, inc=1, device_id=(fi, ei), device_id_type=pl.DeviceIdType.MESH
        )

    signal(sib, e)
    for j in range(1, chips):
        signal(over_there(j) * 2 + core, e)

    @pl.loop(1, n_e)
    def _(k):
        signal(f, lax.rem(e + k, n_e))

    def remote(src, dst, send, recv, fi, ei):
        return pltpu.make_async_remote_copy(
            src_ref=src, dst_ref=dst, send_sem=send, recv_sem=recv,
            device_id=(fi, ei), device_id_type=pl.DeviceIdType.MESH,
        )

    def share(t, j):
        to = sib if j == 0 else over_there(j) * 2 + core
        return remote(wall.at[f, t], wall.at[f, t], w_send.at[j, t], w_recv.at[f, t], to, e)

    def arrival(s, t):
        return remote(wall.at[s, t], wall.at[s, t], w_send.at[0, t], w_recv.at[s, t], sib, e)

    def relay(s, t, j):
        return remote(wall.at[s, t], wall.at[s, t], relay_send.at[j, t], w_recv.at[s, t], sib, e)

    ids_at, gate_at_token[...] = upright(ids[...].astype(F32)), upright(gates[...])
    lanes = lax.broadcasted_iota(jnp.int32, (count, 128), 1)
    first, second = ids_at[:, 0:1].astype(jnp.int32), ids_at[:, 1:2].astype(jnp.int32)
    hit = (lanes == first).astype(F32) + (lanes == second).astype(F32)
    earlier_than = (
        lax.broadcasted_iota(jnp.int32, (count, count), 0)
        > lax.broadcasted_iota(jnp.int32, (count, count), 1)
    ).astype(F32)
    earlier = mul(earlier_than.astype(BF16), hit.astype(BF16), NN)
    spots = lax.broadcasted_iota(jnp.int32, (count, cells), 1)
    gate_at = jnp.zeros((count, cells), F32)
    placed = jnp.zeros((count, cells), F32)
    for k, chosen in enumerate((first, second)):
        slot = jnp.sum(jnp.where(lanes == chosen, earlier, 0.0), axis=1, keepdims=True)
        here = spots == chosen * cap + slot.astype(jnp.int32)
        marks[k] = here.astype(F32).astype(BF16)
        placed += here.astype(F32)
        gate_at += jnp.where(here, gate_at_token[:, k : k + 1], 0.0)
    placing = placed.T.astype(BF16)
    gate_cells = jnp.sum(gate_at.T, axis=1, keepdims=True)

    def part(buf, i):
        return buf.at[pl.ds(pl.multiple_of(i * cap, cap), cap)]

    def exchange(a, src, dst, k):
        to = lax.rem(e + k, n_e)
        return remote(part(src, to), part(dst, e), a_send.at[a, k], a_recv.at[a, k], f, to)

    def arriving(a, src, dst, k):
        frm = lax.rem(e - k + n_e, n_e)
        return remote(part(src, frm), part(dst, frm), a_send.at[a, k], a_recv.at[a, k], f, frm)

    def send_all(a, src, dst):
        @pl.loop(1, n_e)
        def _(k):
            exchange(a, src, dst, k).start()

        own = pl.ds(pl.multiple_of(e * cap, cap), cap)
        dst[own, :] = src[own, :]

    def receive_all(a, src, dst):
        @pl.loop(1, n_e)
        def _(k):
            arriving(a, src, dst, k).wait_recv()

    def sent_all(a, src, dst):
        @pl.loop(1, n_e)
        def _(k):
            exchange(a, src, dst, k).wait_send()

    x_send[...] = mul(placing, tok[...], NN).astype(BF16)
    pl.semaphore_wait(barrier, 1 + (chips - 1) + (n_e - 1))
    for t in range(steps):
        for a in range(2):
            load(t, a).wait()
        for j in range(1, chips):
            share(t, j).start()
        share(t, 0).start()
    send_all(0, x_send, x_rows)
    g_send[...] = (mul(placing, cot[...], NN) * gate_cells).astype(BF16)

    @pl.loop(1, n_e)
    def _(k):
        exchange(0, x_send, x_rows, k).wait_send()
        exchange(1, g_send, g_rows, k).start()

    own_cells = pl.ds(pl.multiple_of(e * cap, cap), cap)
    g_rows[own_cells, :] = g_send[own_cells, :]
    out_acc[...] = jnp.zeros_like(out_acc)
    dx_acc[...] = jnp.zeros_like(dx_acc)

    scale = math.sqrt(2.0 / math.pi)

    def forward(s, t):
        pre = mul(x_rows[...], wall[s, t, 0], NT)
        square = pre * pre
        th = jnp.tanh(scale * pre * (1.0 + 0.044715 * square))
        half = 0.5 * (1.0 + th)
        hidden = (pre * half).astype(BF16)
        hid[s, t] = hidden
        slope[s, t] = half + 0.5 * pre * (1.0 - th * th) * (
            scale * (1.0 + 3.0 * 0.044715 * square)
        )
        out_acc[...] += mul(hidden, wall[s, t, 1], NN)

    receive_all(0, x_send, x_rows)

    @pl.loop(0, steps)
    def _(t):
        forward(f, t)

    @pl.loop(0, steps)
    def _(t):
        arrival(sib, t).wait_recv()
        forward(sib, t)

    def take(j, t):
        s = over_there(j) * 2 + core
        arrival(s, t).wait_recv()
        relay(s, t, j).start()

    def forward_there(j, t):
        forward(over_there(j) * 2 + core, t)
        s = over_there(j) * 2 + 1 - core
        arrival(s, t).wait_recv()
        forward(s, t)

    @pl.loop(1, chips)
    def _(j):
        take(j, 0)
        forward_there(j, 0)

    def back(s, t):
        d_hidden = mul(g_rows[...], wall[s, t, 1], NT)
        d_pre = (d_hidden * slope[s, t]).astype(BF16)
        dx_acc[...] += mul(d_pre, wall[s, t, 0], NN)
        return d_pre

    def weight_grads(s, t, d_pre):
        return mul(d_pre, x_rows[...], TN), mul(hid[s, t], g_rows[...], TN)

    def backward(s, t):
        return weight_grads(s, t, back(s, t))

    def to_sibling(j, t):
        return remote(to_sib.at[j, t], from_sib.at[j, t], s_send.at[j, t], s_recv.at[j, t], sib, e)

    def across(j, t):
        to = over_there(j) * 2 + core
        return remote(to_chip.at[j, t], from_chip.at[j, t], c_send.at[j, t], c_recv.at[j, t], to, e)

    def across_in(j, t):
        frm = before(j) * 2 + core
        return remote(to_chip.at[j, t], from_chip.at[j, t], c_send.at[j, t], c_recv.at[j, t], frm, e)

    def pass_on(j, t, g_in, g_out):
        to_sib[j, t, 0] = g_in.astype(BF16)
        to_sib[j, t, 1] = g_out.astype(BF16)
        to_sibling(j, t).start()

    def backward_there(j, t):
        g_in, g_out = backward(over_there(j) * 2 + 1 - core, t)
        pass_on(j, t, g_in, g_out)
        g_in, g_out = backward(over_there(j) * 2 + core, t)
        to_sibling(j, t).wait_recv()
        to_chip[j, t, 0] = (g_in + from_sib[j, t, 0].astype(F32)).astype(BF16)
        to_chip[j, t, 1] = (g_out + from_sib[j, t, 1].astype(F32)).astype(BF16)
        across(j, t).start()

    receive_all(1, g_send, g_rows)

    @pl.loop(1, chips)
    def _(j):
        backward_there(j, 0)

    @pl.loop(1, steps)
    def _(t):
        @pl.loop(1, chips)
        def _(j):
            take(j, t)

        @pl.loop(1, chips)
        def _(j):
            forward_there(j, t)

    out_send[...] = out_acc[...].astype(BF16)
    send_all(2, out_send, out_back)

    @pl.loop(1, steps)
    def _(t):
        @pl.loop(1, chips)
        def _(j):
            backward_there(j, t)

    for i, s in enumerate((sib, f)):

        @pl.loop(0, steps)
        def _(t, i=i, s=s):
            slopes_on[i, t] = back(s, t)

    dx_send[...] = dx_acc[...].astype(BF16)
    send_all(3, dx_send, dx_back)

    @pl.loop(0, steps)
    def _(t):
        g_in, g_out = weight_grads(sib, t, slopes_on[0, t])
        pass_on(0, t, g_in, g_out)

    @pl.loop(0, steps)
    def _(t):
        g_in, g_out = weight_grads(f, t, slopes_on[1, t])
        rows = pl.ds(pl.multiple_of(t * depth, depth), depth)
        grad_in[rows, :] = g_in
        grad_out[rows, :] = g_out

    @pl.loop(0, steps)
    def _(t):
        to_sibling(0, t).wait_recv()
        rows = pl.ds(pl.multiple_of(t * depth, depth), depth)
        grad_in[rows, :] += from_sib[0, t, 0].astype(F32)
        grad_out[rows, :] += from_sib[0, t, 1].astype(F32)

    receive_all(2, out_send, out_back)
    layer_out[...] = (
        mul(marks[0], out_back[...], NN) * gate_at_token[:, 0:1]
        + mul(marks[1], out_back[...], NN) * gate_at_token[:, 1:2]
    ).astype(BF16)

    @pl.loop(1, chips)
    def _(j):
        @pl.loop(0, steps)
        def _(t):
            across_in(j, t).wait_recv()
            rows = pl.ds(pl.multiple_of(t * depth, depth), depth)
            grad_in[rows, :] += from_chip[j, t, 0].astype(F32)
            grad_out[rows, :] += from_chip[j, t, 1].astype(F32)

    receive_all(3, dx_send, dx_back)
    token_grad[...] = (
        mul(marks[0], dx_back[...], NN) + mul(marks[1], dx_back[...], NN)
    ).astype(BF16)

    sent_all(1, g_send, g_rows)
    sent_all(2, out_send, out_back)
    sent_all(3, dx_send, dx_back)
    for t in range(steps):
        for j in range(chips):
            share(t, j).wait_send()
            to_sibling(j, t).wait_send()
        for j in range(1, chips):
            relay(over_there(j) * 2 + core, t, j).wait_send()
            across(j, t).wait_send()


def settle(*refs):
    for src, dst in zip(refs[:4], refs[4:]):
        dst[...] = src[...]


def per_device(tokens, expert_ids, gate_weights, weight_in, weight_out, cotangent):
    count, width = tokens.shape
    n_f, n_e = lax.axis_size("fsdp"), lax.axis_size("expert")
    cap = 4 * count // n_e
    owned = weight_in.shape[1]
    depth = min(256, owned)
    steps = owned // depth
    rows, chips = n_e * cap, n_f // 2
    vmem = pl.BlockSpec(memory_space=pltpu.VMEM)
    anywhere = pl.BlockSpec(memory_space=pl.ANY)
    dma = pltpu.SemaphoreType.DMA
    wide = pltpu.VMEM((rows, width), BF16)
    total = pltpu.VMEM((rows, width), F32)
    pieces = pltpu.VMEM((chips, steps, 2, depth, width), BF16)
    flops = 12 * rows * width * owned * n_f
    layer_out, token_grad, grad_in, grad_out = pl.pallas_call(
        functools.partial(kernel, n_f, n_e, cap, steps, depth),
        out_shape=(
            jax.ShapeDtypeStruct((count, width), BF16),
            jax.ShapeDtypeStruct((count, width), BF16),
            jax.ShapeDtypeStruct((owned, width), F32),
            jax.ShapeDtypeStruct((owned, width), F32),
        ),
        in_specs=[anywhere, anywhere, vmem, vmem, vmem, vmem],
        out_specs=(vmem, vmem, vmem, vmem),
        scratch_shapes=[
            pltpu.VMEM((n_f, steps, 2, depth, width), BF16),
            wide, wide, wide, wide,
            pltpu.VMEM((n_f, steps, rows, depth), BF16),
            pltpu.VMEM((n_f, steps, rows, depth), F32),
            total, total,
            wide, wide, wide, wide,
            pieces, pieces, pieces, pieces,
            pltpu.VMEM((2, count, rows), BF16),
            pltpu.VMEM((count, 8), F32),
            pltpu.VMEM((2, steps, rows, depth), BF16),
            dma((steps, 2)),
            dma((chips, steps)),
            dma((n_f, steps)),
            dma((chips, steps)),
            dma((4, n_e)),
            dma((4, n_e)),
            dma((chips, steps)),
            dma((chips, steps)),
            dma((chips, steps)),
            dma((chips, steps)),
        ],
        compiler_params=pltpu.CompilerParams(
            collective_id=0, has_side_effects=True, vmem_limit_bytes=58 * 2**20
        ),
        cost_estimate=pl.CostEstimate(
            flops=flops, bytes_accessed=16 * owned * width, transcendentals=rows * owned * n_f
        ),
    )(weight_in[0], weight_out[0], tokens, cotangent, expert_ids.T, gate_weights.T)
    results = (layer_out, token_grad, grad_in, grad_out)
    blocks = [pl.BlockSpec((r.shape[0] // 4, width), lambda i: (i, 0)) for r in results]
    layer_out, token_grad, grad_in, grad_out = pl.pallas_call(
        settle,
        grid=(4,),
        out_shape=tuple(jax.ShapeDtypeStruct(r.shape, r.dtype) for r in results),
        in_specs=blocks,
        out_specs=tuple(blocks),
    )(*results)
    return layer_out, token_grad, grad_in[None], grad_out[None]


def solution(mesh):
    tok, weight = P(("fsdp", "expert"), None), P("expert", "fsdp", None)
    return jax.shard_map(
        per_device,
        mesh=mesh,
        in_specs=(tok, tok, tok, weight, weight, tok),
        out_specs=(tok, tok, weight, weight),
        check_vma=False,
    )
```
